768 devices in a mesh: row: 48 (over z, x), col: 16 (over y, core).
Axes of the slice: x: 4, y: 8, z: 12, core: 2. Of those that a mesh axis runs over, the one named last changes fastest.
Arguments:
- object_field: float32 [4, 2, 6144, 2048], P(None, None, 'row', 'col'), may hold values from -5 to 5
- probe_wave: float32 [2, 128, 128], replicated, may hold values from -6 to 6
- positions: int32 [48, 16, 2, 2], P('row', 'col'), may hold values from 0 to 6143, as said below
- counts: int32 [48, 16], P('row', 'col'), may hold values from 0 to 2, as said below
- measured: float32 [48, 16, 2, 128, 128], P('row', 'col'), may hold values from 0 to 2
Outputs:
- object_grad: float32 [4, 2, 6144, 2048], P(None, None, 'row', 'col')
- probe_grad: float32 [2, 128, 128], replicated
The draws below stay inside these ranges and needn't reach their ends.
Inputs may be any that keep to these rules, and one draw needn't show every extreme that they name: positions[r, c, s] lies inside tile (r, c): its row in r * 128 to (r + 1) * 128 - 1 and its column in c * 128 to (c + 1) * 128 - 1; dead slots hold such positions too. `counts`: some tile has 2 live slots.
All inputs are finite; a program needn't handle non-finite values.
Results may differ from the reference program's by a relative error of at most 0.0003.
Values sent between devices are 32-bit elements; how exact they have to be, the bound alone decides.
No kernel may reach another device: no remote copies, remote signals or barrier semaphores. Data moves between devices by JAX's collectives and lax.ppermute only.
A program may use at most 32 MiB of HBM per device.

```python
import math
import jax
import jax.numpy as jnp
from jax import lax

TR = 128
TC = 128
PROBE = 128
SLICES = 4
CAP = 2
GRID_ROWS = 48
GRID_COLS = 16
NR = 6144
NC = 2048


def draw_positions(key, part):
    row_key = jax.random.fold_in(key, 11)
    col_key = jax.random.fold_in(key, 12)
    shape_all = (GRID_ROWS, GRID_COLS, CAP)
    offset_rows = jax.random.randint(row_key, shape_all, 0, TR)
    offset_cols = jax.random.randint(col_key, shape_all, 0, TC)
    tile_row = lax.broadcasted_iota(jnp.int32, shape_all, 0)
    tile_col = lax.broadcasted_iota(jnp.int32, shape_all, 1)
    centre_rows = tile_row * TR + offset_rows
    centre_cols = tile_col * TC + offset_cols
    return jnp.stack([centre_rows, centre_cols], axis=-1).astype(jnp.int32)


def draw_counts(key, part):
    base_key = jax.random.fold_in(key, 21)
    pick_key = jax.random.fold_in(key, 22)
    drawn = jax.random.randint(base_key, (GRID_ROWS, GRID_COLS), 0, CAP + 1)
    chosen = jax.random.randint(pick_key, (), 0, GRID_ROWS * GRID_COLS)
    flat_index = lax.broadcasted_iota(jnp.int32, (GRID_ROWS, GRID_COLS), 0) * GRID_COLS + lax.broadcasted_iota(jnp.int32, (GRID_ROWS, GRID_COLS), 1)
    return jnp.where(flat_index == chosen, CAP, drawn).astype(jnp.int32)


def shard_levels(rng, shape, shards, smallest, largest):
    factor_of, own = 1.0, jax.random.fold_in(rng, 6)
    for dim, parts in shards:
        steps = jnp.exp(jax.random.uniform(jax.random.fold_in(own, dim), (parts,), jnp.float32, smallest / len(shards), largest / len(shards)))
        factor_of = factor_of * jnp.repeat(steps, shape[dim] // parts).reshape([-1 if axis == dim else 1 for axis in range(len(shape))])
    return factor_of


def bell_draw(rng, extent, width, limit, cuts=(), kind=jnp.bfloat16):
    values = jax.random.normal(rng, extent, jnp.float32) * width
    if len(cuts) > 0:
        values = shard_levels(rng, extent, cuts, -0.22, 0.18) * values
    return jnp.clip(values, min=-limit, max=limit).astype(kind)


def setup_inputs(seed: int = 0) -> dict:
    key_of = jax.random.split(jax.random.key(seed), 6)
    object_field = bell_draw(key_of[0], (SLICES, 2, NR, NC), 0.7, 5.0, ((2, 48), (3, 16)), jnp.float32)
    probe_wave = bell_draw(key_of[1], (2, PROBE, PROBE), 1.0, 6.0, (), jnp.float32)
    positions = draw_positions(jax.random.fold_in(key_of[5], 71), 0)
    counts = draw_counts(jax.random.fold_in(key_of[5], 71), 0)
    measured = jnp.clip(2.0 * jax.random.uniform(key_of[4], (GRID_ROWS, GRID_COLS, CAP, PROBE, PROBE), jnp.float32) ** shard_levels(key_of[4], (GRID_ROWS, GRID_COLS, CAP, PROBE, PROBE), ((0, 48), (1, 16)), -0.2, 0.2), 0.0, 2.0)
    return {"object_field": object_field, "probe_wave": probe_wave, "positions": positions, "counts": counts, "measured": measured}


FRESNEL = 0.01

def matmul_exact(left, right):
    return jnp.dot(left, right, precision=lax.Precision.HIGHEST, preferred_element_type=jnp.float32)

def complex_matmul(left_real, left_imag, right_real, right_imag):
    real_out = matmul_exact(left_real, right_real) - matmul_exact(left_imag, right_imag)
    imag_out = matmul_exact(left_real, right_imag) + matmul_exact(left_imag, right_real)
    return (real_out, imag_out)

def transform(real_part, imag_part, table_real, table_imag):
    first_real, first_imag = complex_matmul(table_real, table_imag, real_part, imag_part)
    return complex_matmul(first_real, first_imag, table_real, table_imag)

def make_tables(points):
    indices = jnp.arange(points, dtype=jnp.int32)
    product = indices[:, None] * indices[None, :] % points
    phase_angle = 2.0 * math.pi / points * product.astype(jnp.float32)
    norm_scale = 1.0 / math.sqrt(points)
    table_real = jnp.cos(phase_angle) * norm_scale
    table_imag = -jnp.sin(phase_angle) * norm_scale
    frequency = jnp.where(indices < points // 2, indices, indices - points).astype(jnp.float32)
    prop_phase = -FRESNEL * (frequency[:, None] ** 2 + frequency[None, :] ** 2)
    return (table_real, table_imag, jnp.cos(prop_phase), jnp.sin(prop_phase))

def position_loss(patch_stack, probe_wave, measured_one, tables):
    table_real, table_imag, prop_real, prop_imag = tables
    wave_real = probe_wave[0]
    wave_imag = probe_wave[1]
    slice_count = patch_stack.shape[0]
    for depth_index in range(slice_count):
        trans_real = patch_stack[depth_index, 0]
        trans_imag = patch_stack[depth_index, 1]
        exit_real = wave_real * trans_real - wave_imag * trans_imag
        exit_imag = wave_real * trans_imag + wave_imag * trans_real
        far_real, far_imag = transform(exit_real, exit_imag, table_real, table_imag)
        if depth_index + 1 < slice_count:
            moved_real = far_real * prop_real - far_imag * prop_imag
            moved_imag = far_real * prop_imag + far_imag * prop_real
            wave_real, wave_imag = transform(moved_real, moved_imag, table_real, -table_imag)
    amplitude = jnp.sqrt(far_real * far_real + far_imag * far_imag + 1.0)
    return jnp.sum((amplitude - measured_one) ** 2)

def reference(object_field, probe_wave, positions, counts, measured):
    slice_count = object_field.shape[0]
    probe_size = probe_wave.shape[-1]
    half_probe = probe_size // 2
    tables = make_tables(probe_size)
    padded = jnp.pad(object_field, ((0, 0), (0, 0), (half_probe, half_probe), (half_probe, half_probe)))
    slot_count = positions.shape[2]
    live_mask = (jnp.arange(slot_count, dtype=jnp.int32)[None, None, :] < counts[:, :, None]).reshape(-1)
    centres = positions.reshape(-1, 2)
    patterns = measured.reshape(-1, probe_size, probe_size)
    gradient = jax.grad(position_loss, argnums=(0, 1))
    anchor = jnp.zeros((), jnp.int32)

    def visit(state_pair, scan_item):
        object_sum, probe_sum = state_pair
        centre, is_live, pattern = scan_item
        starts = (anchor, anchor, centre[0].astype(jnp.int32), centre[1].astype(jnp.int32))
        patch_stack = lax.dynamic_slice(padded, starts, (slice_count, 2, probe_size, probe_size))
        patch_grad, wave_grad = gradient(patch_stack, probe_wave, pattern, tables)
        weight = is_live.astype(jnp.float32)
        current = lax.dynamic_slice(object_sum, starts, (slice_count, 2, probe_size, probe_size))
        object_sum = lax.dynamic_update_slice(object_sum, current + weight * patch_grad, starts)
        return ((object_sum, probe_sum + weight * wave_grad), 0)
    initial = (jnp.zeros(padded.shape, jnp.float32), jnp.zeros(probe_wave.shape, jnp.float32))
    final_pair, unused = lax.scan(visit, initial, (centres, live_mask, patterns))
    object_sum, probe_sum = final_pair
    object_grad = object_sum[:, :, half_probe:-half_probe, half_probe:-half_probe]
    return (object_grad, probe_sum)
```

```python
import jax
import jax.numpy as jnp
import ml_dtypes
import numpy as np
from jax import lax
from jax.experimental import pallas as pl
from jax.experimental.pallas import tpu as pltpu
from jax.sharding import Mesh, PartitionSpec as P

FRESNEL = 0.01
N = 128
H = N // 2
CHIPS_X = 4
CORES = 2
ROW = ("z", "x")
COL = ("y", "c")


def constant_operands():
    k = np.arange(N)
    dft = np.exp(-2j * np.pi / N * (np.outer(k, k) % N)) / np.sqrt(N)
    u = np.where(k < H, k, k - N).astype(np.float64)
    p = np.exp(-1j * FRESNEL * u * u)
    step = dft.conj() @ (p[:, None] * dft)
    out = []
    for a in (step, dft):
        right = np.block([[a.real, a.imag], [-a.imag, a.real]])
        for m in (right, right.T):
            high = m.astype(ml_dtypes.bfloat16)
            low = (m - high.astype(np.float64)).astype(ml_dtypes.bfloat16)
            out += [high, low]
    return np.stack(out)


def split(x):
    high = x.astype(jnp.bfloat16)
    return high, (x - high.astype(jnp.float32)).astype(jnp.bfloat16)


def dot(a, b):
    return jnp.dot(a, b, preferred_element_type=jnp.float32)


def two_sided(wave, right, left):
    x = jnp.concatenate([jnp.concatenate(w, axis=1) for w in wave], axis=0)
    xh, xl = split(x)
    rh, rl = right
    z = dot(jnp.concatenate([xh, xl, xh], axis=1), jnp.concatenate([rh, rh, rl], axis=0))
    z = jnp.concatenate(
        [
            jnp.concatenate([z[:N, :N], z[N:, :N]], axis=1),
            jnp.concatenate([z[:N, N:], z[N:, N:]], axis=1),
        ],
        axis=0,
    )
    zh, zl = split(z)
    lh, ll = left
    y = dot(jnp.concatenate([lh, ll, lh], axis=1), jnp.concatenate([zh, zh, zl], axis=0))
    return [(y[:N, :N], y[N:, :N]), (y[:N, N:], y[N:, N:])]


def lane_mask():
    return lax.broadcasted_iota(jnp.int32, (N, N), 1) < H


def pack_kernel(tile, above, below, to_left, to_right):
    low = lane_mask()
    for k in range(tile.shape[0]):
        for c in range(2):
            t = tile[k, c]
            v = jnp.concatenate([above[k, c], below[k, c]], axis=0)
            to_right[k, c] = jnp.where(low, pltpu.roll(t, H, 1), v)
            to_left[k, c] = jnp.where(low, t, pltpu.roll(v, H, 1))


def turned_rows(x):
    return jnp.concatenate([x[H:], x[:H]], axis=0)


def grad_kernel(
    pos, count, tile, above, below, from_left, from_right, probe, measured, consts,
    own_out, vert_out, left_out, right_out, probe_out, patches, waves,
):
    slices = tile.shape[0]
    low = lane_mask()
    rows = lax.broadcasted_iota(jnp.int32, (N, N), 0)
    cols = lax.broadcasted_iota(jnp.int32, (N, N), 1)
    pair = lambda i: (consts[2 * i], consts[2 * i + 1])
    step, step_t, dft, dft_t = (pair(i) for i in range(4))

    shifts, row_own, col_own = [], [], []
    for s in range(2):
        ry = jnp.bitwise_and(pos[s, 0], N - 1)
        rx = jnp.bitwise_and(pos[s, 1], N - 1)
        shifts.append((ry, rx))
        row_own.append((rows < H) == (rows < ry))
        col_own.append((cols < H) == (cols < rx))

    def candidates(k, c):
        own = pltpu.roll(turned_rows(tile[k, c]), H, 1)
        vert = pltpu.roll(jnp.concatenate([above[k, c], below[k, c]], axis=0), H, 1)
        fl, fr = from_left[k, c], from_right[k, c]
        horiz = turned_rows(jnp.where(low, fl, pltpu.roll(fr, H, 1)))
        corner = jnp.where(low, pltpu.roll(fl, H, 1), fr)
        return own, vert, horiz, corner

    wave = []
    for s in range(2):
        ry, rx = shifts[s]
        wave.append([pltpu.roll(pltpu.roll(probe[c], rx, 1), ry, 0) for c in range(2)])

    for k in range(slices):
        parts = [candidates(k, c) for c in range(2)]
        exit_wave = []
        for s in range(2):
            o = []
            for c in range(2):
                own, vert, horiz, corner = parts[c]
                picked = jnp.where(
                    row_own[s],
                    jnp.where(col_own[s], own, horiz),
                    jnp.where(col_own[s], vert, corner),
                )
                patches[k, s, c] = picked
                waves[k, s, c] = wave[s][c]
                o.append(picked)
            wr, wi = wave[s]
            exit_wave.append((wr * o[0] - wi * o[1], wr * o[1] + wi * o[0]))
        if k + 1 < slices:
            wave = two_sided(exit_wave, step, step_t)
        else:
            far = two_sided(exit_wave, dft, dft_t)

    grad = []
    for s in range(2):
        fr, fi = far[s]
        live = jnp.where(s < count[0, 0], 2.0, 0.0)
        scale = live * (1.0 - measured[s] * lax.rsqrt(fr * fr + fi * fi + 1.0))
        grad.append((scale * fr, scale * fi))
    for k in reversed(range(slices)):
        if k + 1 < slices:
            grad = two_sided(grad, step_t, step)
        else:
            grad = two_sided(grad, dft_t, dft)
        onto_object = [[], []]
        onto_wave = []
        for s in range(2):
            gr, gi = grad[s]
            wr, wi = waves[k, s, 0], waves[k, s, 1]
            pr, pi = patches[k, s, 0], patches[k, s, 1]
            onto_object[0].append(wr * gr + wi * gi)
            onto_object[1].append(wr * gi - wi * gr)
            onto_wave.append((pr * gr + pi * gi, pr * gi - pi * gr))
        grad = onto_wave
        for c in range(2):
            zero = jnp.zeros((N, N), jnp.float32)
            own, vert, horiz, corner = zero, zero, zero, zero
            for s in range(2):
                g = onto_object[c][s]
                inside = jnp.where(row_own[s], g, 0.0)
                outside = jnp.where(row_own[s], 0.0, g)
                own += jnp.where(col_own[s], inside, 0.0)
                horiz += jnp.where(col_own[s], 0.0, inside)
                vert += jnp.where(col_own[s], outside, 0.0)
                corner += jnp.where(col_own[s], 0.0, outside)
            own_out[k, c] = turned_rows(pltpu.roll(own, H, 1))
            vert_out[k, c] = pltpu.roll(vert, H, 1)
            horiz = turned_rows(horiz)
            left_out[k, c] = jnp.where(low, horiz, pltpu.roll(corner, H, 1))
            right_out[k, c] = jnp.where(low, pltpu.roll(horiz, H, 1), corner)

    for c in range(2):
        total = jnp.zeros((N, N), jnp.float32)
        for s in range(2):
            ry, rx = shifts[s]
            back_y = jnp.bitwise_and(N - ry, N - 1)
            back_x = jnp.bitwise_and(N - rx, N - 1)
            total += pltpu.roll(pltpu.roll(grad[s][c], back_x, 1), back_y, 0)
        probe_out[c] = total


def vertical_kernel(vert, from_left, from_right, up_out, down_out):
    low = lane_mask()
    for k in range(vert.shape[0]):
        for c in range(2):
            add = jnp.where(low, pltpu.roll(from_left[k, c], H, 1), from_right[k, c])
            v = vert[k, c] + add
            up_out[k, c] = v[:H]
            down_out[k, c] = v[H:]


def final_kernel(own, from_left, from_right, from_above, from_below, out):
    low = lane_mask()
    for k in range(own.shape[0]):
        for c in range(2):
            add = jnp.where(low, from_left[k, c], pltpu.roll(from_right[k, c], H, 1))
            v = jnp.concatenate([from_above[k, c], from_below[k, c]], axis=0)
            out[k, c] = own[k, c] + add + v


def call(kernel, outs, args, name, scalars=0, scratch=()):
    spec = pl.BlockSpec(memory_space=pltpu.VMEM)
    smem = pl.BlockSpec(memory_space=pltpu.SMEM)
    return pl.pallas_call(
        kernel,
        out_shape=[jax.ShapeDtypeStruct(s, jnp.float32) for s in outs],
        in_specs=[smem] * scalars + [spec] * (len(args) - scalars),
        out_specs=[spec] * len(outs),
        scratch_shapes=list(scratch),
        compiler_params=pltpu.CompilerParams(vmem_limit_bytes=40 * 1024 * 1024),
        name=name,
    )(*args)


def shift(x, axis, forward):
    size = lax.axis_size(axis)
    pairs = [(i, i + 1) if forward else (i + 1, i) for i in range(size - 1)]
    return lax.ppermute(x, axis, pairs)


def exchange(x, axis):
    return lax.all_to_all(x, axis, 0, 0, tiled=True)


def gathered_sum(x, axis):
    n = lax.axis_size(axis)
    rows = x.shape[0]
    parts = exchange(jnp.broadcast_to(x, (n, *x.shape)).reshape(n * rows, N), axis)
    return parts.reshape(n, rows, N).sum(axis=0)


def per_device(object_field, probe_wave, positions, counts, measured):
    slices = object_field.shape[0]
    full = (slices, 2, N, N)
    half = (slices, 2, H, N)
    consts = jnp.asarray(constant_operands())
    with jax.named_scope("object_halo"):
        above = shift(object_field[:, :, H:], ROW, True)
        below = shift(object_field[:, :, :H], ROW, False)
        to_left, to_right = call(
            pack_kernel, [full, full], (object_field, above, below), "pack_halo"
        )
        from_left = shift(to_right, COL, True)
        from_right = shift(to_left, COL, False)
    own, vert, left, right, probe_sum = call(
        grad_kernel,
        [full, full, full, full, (2, N, N)],
        (
            positions[0, 0], counts, object_field, above, below, from_left, from_right,
            probe_wave, measured[0, 0], consts,
        ),
        "slot_gradients",
        scalars=2,
        scratch=[pltpu.VMEM((slices, 2, 2, N, N), jnp.float32) for _ in range(2)],
    )
    with jax.named_scope("gradient_halo"):
        got_right = shift(left, COL, False)
        got_left = shift(right, COL, True)
        up, down = call(
            vertical_kernel, [half, half], (vert, got_left, got_right), "add_vertical"
        )
        got_below = shift(up, ROW, False)
        got_above = shift(down, ROW, True)
        (result,) = call(
            final_kernel, [full], (own, got_left, got_right, got_above, got_below), "add_own"
        )
    with jax.named_scope("probe_sum"):
        groups = lax.axis_size(("x", "c"))
        part = exchange(probe_sum.reshape(2 * N, N), ("x", "c"))
        part = part.reshape(groups, 2 * N // groups, N).sum(axis=0)
        part = gathered_sum(part, "y")
        part = gathered_sum(part, "z")
        spread = jnp.broadcast_to(part, (groups, *part.shape)).reshape(2 * N, N)
        probe_grad = exchange(spread, ("x", "c")).reshape(2, N, N)
    return (result, probe_grad)


def solution(mesh):
    rows, cols = mesh.devices.shape
    devices = mesh.devices.reshape(rows // CHIPS_X, CHIPS_X, cols // CORES, CORES)
    fine = Mesh(devices, ("z", "x", "y", "c"))
    in_specs = (
        P(None, None, ROW, COL),
        P(),
        P(ROW, COL, None, None),
        P(ROW, COL),
        P(ROW, COL, None, None, None),
    )
    out_specs = (P(None, None, ROW, COL), P())
    return jax.shard_map(
        per_device, mesh=fine, in_specs=in_specs, out_specs=out_specs, check_vma=False
    )
```

```python
import jax
import jax.numpy as jnp
import ml_dtypes
import numpy as np
from jax import lax
from jax.experimental import pallas as pl
from jax.experimental.pallas import tpu as pltpu
from jax.sharding import Mesh, PartitionSpec as P

FRESNEL = 0.01
N = 128
H = N // 2
CHIPS_X = 4
CORES = 2
ROW = ("z", "x")
COL = ("y", "c")


def constant_operands():
    k = np.arange(N)
    dft = np.exp(-2j * np.pi / N * (np.outer(k, k) % N)) / np.sqrt(N)
    u = np.where(k < H, k, k - N).astype(np.float64)
    p = np.exp(-1j * FRESNEL * u * u)
    step = dft.conj() @ (p[:, None] * dft)
    out = []
    for m in (step.real, step.imag, dft.real, dft.imag):
        high = m.astype(ml_dtypes.bfloat16)
        out += [high, (m - high.astype(np.float64)).astype(ml_dtypes.bfloat16)]
    return np.stack(out)


def split(x):
    high = x.astype(jnp.bfloat16)
    return high, (x - high.astype(jnp.float32)).astype(jnp.bfloat16)


def dot(a, b):
    return jnp.dot(a, b, preferred_element_type=jnp.float32)


def two_sided(wave, right, left):
    x = jnp.concatenate([jnp.concatenate(w, axis=1) for w in wave], axis=0)
    xh, xl = split(x)
    rh, rl = right
    z = dot(jnp.concatenate([xh, xl, xh], axis=1), jnp.concatenate([rh, rh, rl], axis=0))
    z = jnp.concatenate(
        [
            jnp.concatenate([z[:N, :N], z[N:, :N]], axis=1),
            jnp.concatenate([z[:N, N:], z[N:, N:]], axis=1),
        ],
        axis=0,
    )
    zh, zl = split(z)
    lh, ll = left
    y = dot(jnp.concatenate([lh, ll, lh], axis=1), jnp.concatenate([zh, zh, zl], axis=0))
    return [(y[:N, :N], y[N:, :N]), (y[:N, N:], y[N:, N:])]


def lane_mask():
    return lax.broadcasted_iota(jnp.int32, (N, N), 1) < H


def pack_columns(x, to_left, to_right, k, c):
    low = lax.broadcasted_iota(jnp.int32, (H, N), 1) < H
    upper, lower = x[:H], x[H:]
    to_right[k, c] = jnp.where(low, pltpu.roll(upper, H, 1), lower)
    to_left[k, c] = jnp.where(low, upper, pltpu.roll(lower, H, 1))


def unpack_columns(from_left, from_right):
    low = lax.broadcasted_iota(jnp.int32, (H, N), 1) < H
    upper = jnp.where(low, from_left, pltpu.roll(from_right, H, 1))
    lower = jnp.where(low, pltpu.roll(from_left, H, 1), from_right)
    return jnp.concatenate([upper, lower], axis=0)


def edges_kernel(tile, to_up, to_down, to_left, to_right):
    for k in range(tile.shape[0]):
        for c in range(2):
            t = tile[k, c]
            to_up[k, c] = t[:H]
            to_down[k, c] = t[H:]
            pack_columns(t, to_left, to_right, k, c)


def corners_kernel(above, below, to_left, to_right):
    for k in range(above.shape[0]):
        for c in range(2):
            v = jnp.concatenate([above[k, c], below[k, c]], axis=0)
            pack_columns(v, to_left, to_right, k, c)


def turned_rows(x):
    return jnp.concatenate([x[H:], x[:H]], axis=0)


def grad_kernel(
    pos, count, tile, above, below, from_left, from_right, corner_left, corner_right,
    probe, measured, consts,
    own_out, vert_out, horiz_out, corner_out, probe_out, patches, waves,
):
    slices = tile.shape[0]
    low = lane_mask()
    rows = lax.broadcasted_iota(jnp.int32, (N, N), 0)
    cols = lax.broadcasted_iota(jnp.int32, (N, N), 1)
    def operator(i):
        right, left = [], []
        for term in range(2):
            real, imag = consts[4 * i + term], consts[4 * i + 2 + term]
            row = jnp.concatenate([real, imag], axis=1)
            col = jnp.concatenate([real, -imag], axis=1)
            right.append(jnp.concatenate([row, jnp.concatenate([-imag, real], axis=1)], axis=0))
            left.append(jnp.concatenate([col, jnp.concatenate([imag, real], axis=1)], axis=0))
        return right, left

    (step, step_t), (dft, dft_t) = operator(0), operator(1)

    shifts, row_own, col_own = [], [], []
    for s in range(2):
        ry = jnp.bitwise_and(pos[0, 0, s, 0], N - 1)
        rx = jnp.bitwise_and(pos[0, 0, s, 1], N - 1)
        shifts.append((ry, rx))
        row_own.append((rows < H) == (rows < ry))
        col_own.append((cols < H) == (cols < rx))

    def candidates(k, c):
        own = pltpu.roll(turned_rows(tile[k, c]), H, 1)
        vert = pltpu.roll(jnp.concatenate([above[k, c], below[k, c]], axis=0), H, 1)
        horiz = turned_rows(unpack_columns(from_left[k, c], from_right[k, c]))
        corner = unpack_columns(corner_left[k, c], corner_right[k, c])
        return own, vert, horiz, corner

    wave = []
    for s in range(2):
        ry, rx = shifts[s]
        wave.append([pltpu.roll(pltpu.roll(probe[c], rx, 1), ry, 0) for c in range(2)])

    for k in range(slices):
        parts = [candidates(k, c) for c in range(2)]
        exit_wave = []
        for s in range(2):
            o = []
            for c in range(2):
                own, vert, horiz, corner = parts[c]
                picked = jnp.where(
                    row_own[s],
                    jnp.where(col_own[s], own, horiz),
                    jnp.where(col_own[s], vert, corner),
                )
                patches[k, s, c] = picked
                waves[k, s, c] = wave[s][c]
                o.append(picked)
            wr, wi = wave[s]
            exit_wave.append((wr * o[0] - wi * o[1], wr * o[1] + wi * o[0]))
        if k + 1 < slices:
            wave = two_sided(exit_wave, step, step_t)
        else:
            far = two_sided(exit_wave, dft, dft_t)

    grad = []
    for s in range(2):
        fr, fi = far[s]
        live = jnp.where(s < count[0, 0], 2.0, 0.0)
        scale = live * (1.0 - measured[s] * lax.rsqrt(fr * fr + fi * fi + 1.0))
        grad.append((scale * fr, scale * fi))
    for k in reversed(range(slices)):
        if k + 1 < slices:
            grad = two_sided(grad, step_t, step)
        else:
            grad = two_sided(grad, dft_t, dft)
        onto_object = [[], []]
        onto_wave = []
        for s in range(2):
            gr, gi = grad[s]
            wr, wi = waves[k, s, 0], waves[k, s, 1]
            pr, pi = patches[k, s, 0], patches[k, s, 1]
            onto_object[0].append(wr * gr + wi * gi)
            onto_object[1].append(wr * gi - wi * gr)
            onto_wave.append((pr * gr + pi * gi, pr * gi - pi * gr))
        grad = onto_wave
        for c in range(2):
            zero = jnp.zeros((N, N), jnp.float32)
            own, vert, horiz, corner = zero, zero, zero, zero
            for s in range(2):
                g = onto_object[c][s]
                inside = jnp.where(row_own[s], g, 0.0)
                outside = jnp.where(row_own[s], 0.0, g)
                own += jnp.where(col_own[s], inside, 0.0)
                horiz += jnp.where(col_own[s], 0.0, inside)
                vert += jnp.where(col_own[s], outside, 0.0)
                corner += jnp.where(col_own[s], 0.0, outside)
            own_out[k, c] = own
            vert_out[k, c] = vert
            horiz_out[k, c] = horiz
            corner_out[k, c] = corner

    for c in range(2):
        total = jnp.zeros((N, N), jnp.float32)
        for s in range(2):
            ry, rx = shifts[s]
            back_y = jnp.bitwise_and(N - ry, N - 1)
            back_x = jnp.bitwise_and(N - rx, N - 1)
            total += pltpu.roll(pltpu.roll(grad[s][c], back_x, 1), back_y, 0)
        probe_out[c] = total


def sides_kernel(horiz_in, corner_in, left_out, right_out):
    low = lane_mask()
    for k in range(horiz_in.shape[0]):
        for c in range(2):
            horiz, corner = turned_rows(horiz_in[k, c]), corner_in[k, c]
            left_out[k, c] = jnp.where(low, horiz, pltpu.roll(corner, H, 1))
            right_out[k, c] = jnp.where(low, pltpu.roll(horiz, H, 1), corner)


def vertical_kernel(vert, from_left, from_right, up_out, down_out):
    low = lane_mask()
    for k in range(vert.shape[0]):
        for c in range(2):
            add = jnp.where(low, pltpu.roll(from_left[k, c], H, 1), from_right[k, c])
            v = pltpu.roll(vert[k, c], H, 1) + add
            up_out[k, c] = v[:H]
            down_out[k, c] = v[H:]


def final_kernel(own, from_left, from_right, from_above, from_below, out):
    low = lane_mask()
    for k in range(own.shape[0]):
        for c in range(2):
            add = jnp.where(low, from_left[k, c], pltpu.roll(from_right[k, c], H, 1))
            v = jnp.concatenate([from_above[k, c], from_below[k, c]], axis=0)
            out[k, c] = turned_rows(pltpu.roll(own[k, c], H, 1)) + add + v


def call(kernel, outs, args, name, scalars=0, scratch=(), vmem=4, flops=0):
    spec = pl.BlockSpec(memory_space=pltpu.VMEM)
    smem = pl.BlockSpec(memory_space=pltpu.SMEM)
    return pl.pallas_call(
        kernel,
        out_shape=[jax.ShapeDtypeStruct(s, jnp.float32) for s in outs],
        in_specs=[smem] * scalars + [spec] * (len(args) - scalars),
        out_specs=[spec] * len(outs),
        scratch_shapes=list(scratch),
        compiler_params=pltpu.CompilerParams(vmem_limit_bytes=vmem * 1024 * 1024),
        cost_estimate=pl.CostEstimate(
            flops=flops,
            bytes_accessed=sum(4 * int(np.prod(s)) for s in outs) + sum(x.nbytes for x in args),
            transcendentals=0,
        ),
        name=name,
    )(*args)


def shift(x, axis, forward):
    size = lax.axis_size(axis)
    pairs = [(i, i + 1) if forward else (i + 1, i) for i in range(size - 1)]
    return lax.ppermute(x, axis, pairs)


def exchange(x, axis):
    return lax.all_to_all(x, axis, 0, 0, tiled=True)


def gathered_sum(x, axis):
    n = lax.axis_size(axis)
    rows = x.shape[0]
    parts = exchange(jnp.broadcast_to(x, (n, *x.shape)).reshape(n * rows, N), axis)
    return parts.reshape(n, rows, N).sum(axis=0)


def per_device(object_field, probe_wave, positions, counts, measured):
    slices = object_field.shape[0]
    full = (slices, 2, N, N)
    half = (slices, 2, H, N)
    consts = jnp.asarray(constant_operands())
    with jax.named_scope("object_halo"):
        to_up, to_down, to_left, to_right = call(
            edges_kernel, [half] * 4, (object_field,), "pack_edges"
        )
        above = shift(to_down, ROW, True)
        below = shift(to_up, ROW, False)
        from_left = shift(to_right, COL, True)
        from_right = shift(to_left, COL, False)
        to_left, to_right = call(corners_kernel, [half] * 2, (above, below), "pack_corners")
        corner_left = shift(to_right, COL, True)
        corner_right = shift(to_left, COL, False)
    own, vert, horiz, corner, probe_sum = call(
        grad_kernel,
        [full, full, full, full, (2, N, N)],
        (
            positions, counts, object_field, above, below, from_left, from_right,
            corner_left, corner_right, probe_wave, measured[0, 0], consts,
        ),
        "slot_gradients",
        scalars=2,
        vmem=16,
        flops=16 * 6 * (2 * N) ** 3,
        scratch=[pltpu.VMEM((slices, 2, 2, N, N), jnp.float32) for _ in range(2)],
    )
    with jax.named_scope("gradient_halo"):
        left, right = call(sides_kernel, [full] * 2, (horiz, corner), "pack_sides")
        got_right = shift(left, COL, False)
        got_left = shift(right, COL, True)
        up, down = call(
            vertical_kernel, [half, half], (vert, got_left, got_right), "add_vertical"
        )
        got_below = shift(up, ROW, False)
        got_above = shift(down, ROW, True)
        (result,) = call(
            final_kernel, [full], (own, got_left, got_right, got_above, got_below), "add_own"
        )
    with jax.named_scope("probe_sum"):
        plane = ("x", "y", "c")
        groups = lax.axis_size(plane)
        part = exchange(probe_sum.reshape(2 * N, N), plane)
        part = part.reshape(groups, 2 * N // groups, N).sum(axis=0)
        part = gathered_sum(part, "z")
        spread = jnp.broadcast_to(part, (groups, *part.shape)).reshape(2 * N, N)
        probe_grad = exchange(spread, plane).reshape(2, N, N)
    return (result, probe_grad)


def solution(mesh):
    rows, cols = mesh.devices.shape
    devices = mesh.devices.reshape(rows // CHIPS_X, CHIPS_X, cols // CORES, CORES)
    fine = Mesh(devices, ("z", "x", "y", "c"))
    in_specs = (
        P(None, None, ROW, COL),
        P(),
        P(ROW, COL, None, None),
        P(ROW, COL),
        P(ROW, COL, None, None, None),
    )
    out_specs = (P(None, None, ROW, COL), P())
    return jax.shard_map(
        per_device, mesh=fine, in_specs=in_specs, out_specs=out_specs, check_vma=False
    )
```

```python
import jax
import jax.numpy as jnp
import ml_dtypes
import numpy as np
from jax import lax
from jax.experimental import pallas as pl
from jax.experimental.pallas import tpu as pltpu
from jax.sharding import Mesh, PartitionSpec as P

FRESNEL = 0.01
N = 128
H = N // 2
CHIPS_X = 4
CORES = 2
ROW = ("z", "x")
COL = ("y", "c")


def constant_operands():
    k = np.arange(N)
    dft = np.exp(-2j * np.pi / N * (np.outer(k, k) % N)) / np.sqrt(N)
    u = np.where(k < H, k, k - N).astype(np.float64)
    p = np.exp(-1j * FRESNEL * u * u)
    step = dft.conj() @ (p[:, None] * dft)
    out = []
    for m in (step.real, step.imag, dft.real, dft.imag):
        high = m.astype(ml_dtypes.bfloat16)
        out += [high, (m - high.astype(np.float64)).astype(ml_dtypes.bfloat16)]
    return np.stack(out)


def split(x):
    high = x.astype(jnp.bfloat16)
    return high, (x - high.astype(jnp.float32)).astype(jnp.bfloat16)


def dot(a, b):
    return jnp.dot(a, b, preferred_element_type=jnp.float32)


def two_sided(wave, right, left):
    x = jnp.concatenate([jnp.concatenate(w, axis=1) for w in wave], axis=0)
    xh, xl = split(x)
    rh, rl = right
    z = dot(jnp.concatenate([xh, xl, xh], axis=1), jnp.concatenate([rh, rh, rl], axis=0))
    z = jnp.concatenate(
        [
            jnp.concatenate([z[:N, :N], z[N:, :N]], axis=1),
            jnp.concatenate([z[:N, N:], z[N:, N:]], axis=1),
        ],
        axis=0,
    )
    zh, zl = split(z)
    lh, ll = left
    y = dot(jnp.concatenate([lh, ll, lh], axis=1), jnp.concatenate([zh, zh, zl], axis=0))
    return [(y[:N, :N], y[N:, :N]), (y[:N, N:], y[N:, N:])]


def lane_mask():
    return lax.broadcasted_iota(jnp.int32, (N, N), 1) < H


def pack_columns(x, to_left, to_right, k, c):
    low = lax.broadcasted_iota(jnp.int32, (H, N), 1) < H
    upper, lower = x[:H], x[H:]
    to_right[k, c] = jnp.where(low, pltpu.roll(upper, H, 1), lower)
    to_left[k, c] = jnp.where(low, upper, pltpu.roll(lower, H, 1))


def unpack_columns(from_left, from_right):
    low = lax.broadcasted_iota(jnp.int32, (H, N), 1) < H
    upper = jnp.where(low, from_left, pltpu.roll(from_right, H, 1))
    lower = jnp.where(low, pltpu.roll(from_left, H, 1), from_right)
    return jnp.concatenate([upper, lower], axis=0)


def edges_kernel(tile, to_up, to_down, to_left, to_right):
    for k in range(tile.shape[0]):
        for c in range(2):
            t = tile[k, c]
            to_up[k, c] = t[:H]
            to_down[k, c] = t[H:]
            pack_columns(t, to_left, to_right, k, c)


def corners_kernel(above, below, to_left, to_right):
    for k in range(above.shape[0]):
        for c in range(2):
            v = jnp.concatenate([above[k, c], below[k, c]], axis=0)
            pack_columns(v, to_left, to_right, k, c)


def turned_rows(x):
    return jnp.concatenate([x[H:], x[:H]], axis=0)


def grad_kernel(
    pos, count, tile, above, below, from_left, from_right, corner_left, corner_right,
    probe, measured, consts,
    own_out, vert_out, horiz_out, corner_out, probe_out, patches, waves,
):
    slices = tile.shape[0]
    low = lane_mask()
    rows = lax.broadcasted_iota(jnp.int32, (N, N), 0)
    cols = lax.broadcasted_iota(jnp.int32, (N, N), 1)
    def operator(i):
        right, left = [], []
        for term in range(2):
            real, imag = consts[4 * i + term], consts[4 * i + 2 + term]
            row = jnp.concatenate([real, imag], axis=1)
            col = jnp.concatenate([real, -imag], axis=1)
            right.append(jnp.concatenate([row, jnp.concatenate([-imag, real], axis=1)], axis=0))
            left.append(jnp.concatenate([col, jnp.concatenate([imag, real], axis=1)], axis=0))
        return right, left

    (step, step_t), (dft, dft_t) = operator(0), operator(1)

    shifts, row_own, col_own = [], [], []
    for s in range(2):
        ry = jnp.bitwise_and(pos[0, 0, s, 0], N - 1)
        rx = jnp.bitwise_and(pos[0, 0, s, 1], N - 1)
        shifts.append((ry, rx))
        row_own.append((rows < H) == (rows < ry))
        col_own.append((cols < H) == (cols < rx))

    def candidates(k, c):
        own = pltpu.roll(turned_rows(tile[k, c]), H, 1)
        vert = pltpu.roll(jnp.concatenate([above[k, c], below[k, c]], axis=0), H, 1)
        horiz = turned_rows(unpack_columns(from_left[k, c], from_right[k, c]))
        corner = unpack_columns(corner_left[k, c], corner_right[k, c])
        return own, vert, horiz, corner

    wave = []
    for s in range(2):
        ry, rx = shifts[s]
        wave.append([pltpu.roll(pltpu.roll(probe[c], rx, 1), ry, 0) for c in range(2)])

    for k in range(slices):
        parts = [candidates(k, c) for c in range(2)]
        exit_wave = []
        for s in range(2):
            o = []
            for c in range(2):
                own, vert, horiz, corner = parts[c]
                picked = jnp.where(
                    row_own[s],
                    jnp.where(col_own[s], own, horiz),
                    jnp.where(col_own[s], vert, corner),
                )
                patches[k, s, c] = picked
                waves[k, s, c] = wave[s][c]
                o.append(picked)
            wr, wi = wave[s]
            exit_wave.append((wr * o[0] - wi * o[1], wr * o[1] + wi * o[0]))
        if k + 1 < slices:
            wave = two_sided(exit_wave, step, step_t)
        else:
            far = two_sided(exit_wave, dft, dft_t)

    grad = []
    for s in range(2):
        fr, fi = far[s]
        live = jnp.where(s < count[0, 0], 2.0, 0.0)
        scale = live * (1.0 - measured[s] * lax.rsqrt(fr * fr + fi * fi + 1.0))
        grad.append((scale * fr, scale * fi))
    for k in reversed(range(slices)):
        if k + 1 < slices:
            grad = two_sided(grad, step_t, step)
        else:
            grad = two_sided(grad, dft_t, dft)
        onto_object = [[], []]
        onto_wave = []
        for s in range(2):
            gr, gi = grad[s]
            wr, wi = waves[k, s, 0], waves[k, s, 1]
            pr, pi = patches[k, s, 0], patches[k, s, 1]
            onto_object[0].append(wr * gr + wi * gi)
            onto_object[1].append(wr * gi - wi * gr)
            onto_wave.append((pr * gr + pi * gi, pr * gi - pi * gr))
        grad = onto_wave
        for c in range(2):
            zero = jnp.zeros((N, N), jnp.float32)
            own, vert, horiz, corner = zero, zero, zero, zero
            for s in range(2):
                g = onto_object[c][s]
                inside = jnp.where(row_own[s], g, 0.0)
                outside = jnp.where(row_own[s], 0.0, g)
                own += jnp.where(col_own[s], inside, 0.0)
                horiz += jnp.where(col_own[s], 0.0, inside)
                vert += jnp.where(col_own[s], outside, 0.0)
                corner += jnp.where(col_own[s], 0.0, outside)
            own_out[k, c] = own
            vert_out[k, c] = vert
            horiz_out[k, c] = horiz
            corner_out[k, c] = corner

    for c in range(2):
        total = jnp.zeros((N, N), jnp.float32)
        for s in range(2):
            ry, rx = shifts[s]
            back_y = jnp.bitwise_and(N - ry, N - 1)
            back_x = jnp.bitwise_and(N - rx, N - 1)
            total += pltpu.roll(pltpu.roll(grad[s][c], back_x, 1), back_y, 0)
        probe_out[c] = total


def sides_kernel(horiz_in, corner_in, left_out, right_out):
    low = lane_mask()
    for k in range(horiz_in.shape[0]):
        for c in range(2):
            horiz, corner = turned_rows(horiz_in[k, c]), corner_in[k, c]
            left_out[k, c] = jnp.where(low, horiz, pltpu.roll(corner, H, 1))
            right_out[k, c] = jnp.where(low, pltpu.roll(horiz, H, 1), corner)


def vertical_kernel(vert, from_left, from_right, up_out, down_out):
    low = lane_mask()
    for k in range(vert.shape[0]):
        for c in range(2):
            add = jnp.where(low, pltpu.roll(from_left[k, c], H, 1), from_right[k, c])
            v = pltpu.roll(vert[k, c], H, 1) + add
            up_out[k, c] = v[:H]
            down_out[k, c] = v[H:]


def final_kernel(own, from_left, from_right, from_above, from_below, out):
    low = lane_mask()
    for k in range(own.shape[0]):
        for c in range(2):
            add = jnp.where(low, from_left[k, c], pltpu.roll(from_right[k, c], H, 1))
            v = jnp.concatenate([from_above[k, c], from_below[k, c]], axis=0)
            out[k, c] = turned_rows(pltpu.roll(own[k, c], H, 1)) + add + v


def call(kernel, outs, args, name, scalars=0, scratch=(), vmem=4, flops=0):
    spec = pl.BlockSpec(memory_space=pltpu.VMEM)
    smem = pl.BlockSpec(memory_space=pltpu.SMEM)
    return pl.pallas_call(
        kernel,
        out_shape=[jax.ShapeDtypeStruct(s, jnp.float32) for s in outs],
        in_specs=[smem] * scalars + [spec] * (len(args) - scalars),
        out_specs=[spec] * len(outs),
        scratch_shapes=list(scratch),
        compiler_params=pltpu.CompilerParams(vmem_limit_bytes=vmem * 1024 * 1024),
        cost_estimate=pl.CostEstimate(
            flops=flops,
            bytes_accessed=sum(4 * int(np.prod(s)) for s in outs) + sum(x.nbytes for x in args),
            transcendentals=0,
        ),
        name=name,
    )(*args)


def shift(x, axis, forward):
    size = lax.axis_size(axis)
    pairs = [(i, i + 1) if forward else (i + 1, i) for i in range(size - 1)]
    return lax.ppermute(x, axis, pairs)


def exchange(x, axis):
    return lax.all_to_all(x, axis, 0, 0, tiled=True)


def gathered_sum(x, axis):
    n = lax.axis_size(axis)
    rows = x.shape[0]
    parts = exchange(jnp.broadcast_to(x, (n, *x.shape)).reshape(n * rows, N), axis)
    return parts.reshape(n, rows, N).sum(axis=0)


def per_device(object_field, probe_wave, positions, counts, measured):
    slices = object_field.shape[0]
    full = (slices, 2, N, N)
    half = (slices, 2, H, N)
    consts = jnp.asarray(constant_operands())
    with jax.named_scope("object_halo"):
        to_up, to_down, to_left, to_right = call(
            edges_kernel, [half] * 4, (object_field,), "pack_edges"
        )
        above = shift(to_down, ROW, True)
        below = shift(to_up, ROW, False)
        from_left = shift(to_right, COL, True)
        from_right = shift(to_left, COL, False)
        to_left, to_right = call(corners_kernel, [half] * 2, (above, below), "pack_corners")
        corner_left = shift(to_right, COL, True)
        corner_right = shift(to_left, COL, False)
    own, vert, horiz, corner, probe_sum = call(
        grad_kernel,
        [full, full, full, full, (2, N, N)],
        (
            positions, counts, object_field, above, below, from_left, from_right,
            corner_left, corner_right, probe_wave, measured[0, 0], consts,
        ),
        "slot_gradients",
        scalars=2,
        vmem=16,
        flops=16 * 6 * (2 * N) ** 3,
        scratch=[pltpu.VMEM((slices, 2, 2, N, N), jnp.float32) for _ in range(2)],
    )
    with jax.named_scope("gradient_halo"):
        left, right = call(sides_kernel, [full] * 2, (horiz, corner), "pack_sides")
        got_right = shift(left, COL, False)
        got_left = shift(right, COL, True)
        up, down = call(
            vertical_kernel, [half, half], (vert, got_left, got_right), "add_vertical"
        )
        got_below = shift(up, ROW, False)
        got_above = shift(down, ROW, True)
        (result,) = call(
            final_kernel, [full], (own, got_left, got_right, got_above, got_below), "add_own"
        )
    with jax.named_scope("probe_sum"):
        near = ("x", "c")
        groups = lax.axis_size(near)
        part = exchange(probe_sum.reshape(2 * N, N), near)
        part = part.reshape(groups, 2 * N // groups, N).sum(axis=0)
        part = gathered_sum(part, "y")
        part = gathered_sum(part, "z")
        spread = jnp.broadcast_to(part, (groups, *part.shape)).reshape(2 * N, N)
        probe_grad = exchange(spread, near).reshape(2, N, N)
    return (result, probe_grad)


def solution(mesh):
    rows, cols = mesh.devices.shape
    devices = mesh.devices.reshape(rows // CHIPS_X, CHIPS_X, cols // CORES, CORES)
    fine = Mesh(devices, ("z", "x", "y", "c"))
    in_specs = (
        P(None, None, ROW, COL),
        P(),
        P(ROW, COL, None, None),
        P(ROW, COL),
        P(ROW, COL, None, None, None),
    )
    out_specs = (P(None, None, ROW, COL), P())
    return jax.shard_map(
        per_device, mesh=fine, in_specs=in_specs, out_specs=out_specs, check_vma=False
    )
```

```python
import jax
import jax.numpy as jnp
import ml_dtypes
import numpy as np
from jax import lax
from jax.experimental import pallas as pl
from jax.experimental.pallas import tpu as pltpu
from jax.sharding import Mesh, PartitionSpec as P

FRESNEL = 0.01
N = 128
H = N // 2
CHIPS_X = 4
CORES = 2
ROW = ("z", "x")
COL = ("y", "c")


def constant_operands():
    k = np.arange(N)
    dft = np.exp(-2j * np.pi / N * (np.outer(k, k) % N)) / np.sqrt(N)
    u = np.where(k < H, k, k - N).astype(np.float64)
    p = np.exp(-1j * FRESNEL * u * u)
    step = dft.conj() @ (p[:, None] * dft)
    out = []
    for m in (step.real, step.imag, dft.real, dft.imag):
        high = m.astype(ml_dtypes.bfloat16)
        out += [high, (m - high.astype(np.float64)).astype(ml_dtypes.bfloat16)]
    return np.stack(out)


def split(x):
    high = x.astype(jnp.bfloat16)
    return high, (x - high.astype(jnp.float32)).astype(jnp.bfloat16)


def dot(a, b):
    return jnp.dot(a, b, preferred_element_type=jnp.float32)


def two_sided(wave, right, left):
    x = jnp.concatenate([jnp.concatenate(w, axis=1) for w in wave], axis=0)
    xh, xl = split(x)
    rh, rl = right
    z = dot(jnp.concatenate([xh, xl, xh], axis=1), jnp.concatenate([rh, rh, rl], axis=0))
    z = jnp.concatenate(
        [
            jnp.concatenate([z[:N, :N], z[N:, :N]], axis=1),
            jnp.concatenate([z[:N, N:], z[N:, N:]], axis=1),
        ],
        axis=0,
    )
    zh, zl = split(z)
    lh, ll = left
    y = dot(jnp.concatenate([lh, ll, lh], axis=1), jnp.concatenate([zh, zh, zl], axis=0))
    return [(y[:N, :N], y[N:, :N]), (y[:N, N:], y[N:, N:])]


def lane_mask():
    return lax.broadcasted_iota(jnp.int32, (N, N), 1) < H


def pack_columns(x):
    low = lax.broadcasted_iota(jnp.int32, (H, N), 1) < H
    upper, lower = x[:H], x[H:]
    to_right = jnp.where(low, pltpu.roll(upper, H, 1), lower)
    return jnp.where(low, upper, pltpu.roll(lower, H, 1)), to_right


def unpack_columns(from_left, from_right):
    low = lax.broadcasted_iota(jnp.int32, (H, N), 1) < H
    upper = jnp.where(low, from_left, pltpu.roll(from_right, H, 1))
    lower = jnp.where(low, pltpu.roll(from_left, H, 1), from_right)
    return jnp.concatenate([upper, lower], axis=0)


def even(axis):
    return jnp.full((H, N), jnp.bitwise_and(lax.axis_index(axis), 1), jnp.int32) == 0


def sort(is_even, before, after):
    return jnp.where(is_even, before, after), jnp.where(is_even, after, before)


def edges_kernel(tile, row_across, row_mate, col_across, col_mate):
    row_even, col_even = even("x"), even("c")
    for k in range(tile.shape[0]):
        for c in range(2):
            t = tile[k, c]
            row_across[k, c], row_mate[k, c] = sort(row_even, t[:H], t[H:])
            col_across[k, c], col_mate[k, c] = sort(col_even, *pack_columns(t))


def corners_kernel(row_across, row_mate, col_across, col_mate):
    row_even, col_even = even("x"), even("c")
    for k in range(row_across.shape[0]):
        for c in range(2):
            v = jnp.concatenate(sort(row_even, row_across[k, c], row_mate[k, c]), axis=0)
            col_across[k, c], col_mate[k, c] = sort(col_even, *pack_columns(v))


def turned_rows(x):
    return jnp.concatenate([x[H:], x[:H]], axis=0)


def grad_kernel(
    pos, count, tile, row_across, row_mate, col_across, col_mate, corner_across, corner_mate,
    probe, measured, consts,
    own_out, vert_out, horiz_out, corner_out, probe_out, patches, waves,
):
    slices = tile.shape[0]
    row_even, col_even = even("x"), even("c")
    rows = lax.broadcasted_iota(jnp.int32, (N, N), 0)
    cols = lax.broadcasted_iota(jnp.int32, (N, N), 1)
    def operator(i):
        right, left = [], []
        for term in range(2):
            real, imag = consts[4 * i + term], consts[4 * i + 2 + term]
            row = jnp.concatenate([real, imag], axis=1)
            col = jnp.concatenate([real, -imag], axis=1)
            right.append(jnp.concatenate([row, jnp.concatenate([-imag, real], axis=1)], axis=0))
            left.append(jnp.concatenate([col, jnp.concatenate([imag, real], axis=1)], axis=0))
        return right, left

    (step, step_t), (dft, dft_t) = operator(0), operator(1)

    shifts, row_own, col_own = [], [], []
    for s in range(2):
        ry = jnp.bitwise_and(pos[0, 0, s, 0], N - 1)
        rx = jnp.bitwise_and(pos[0, 0, s, 1], N - 1)
        shifts.append((ry, rx))
        row_own.append((rows < H) == (rows < ry))
        col_own.append((cols < H) == (cols < rx))

    def candidates(k, c):
        own = pltpu.roll(turned_rows(tile[k, c]), H, 1)
        vert = sort(row_even, row_across[k, c], row_mate[k, c])
        vert = pltpu.roll(jnp.concatenate(vert, axis=0), H, 1)
        horiz = sort(col_even, col_across[k, c], col_mate[k, c])
        horiz = turned_rows(unpack_columns(*horiz))
        corner = sort(col_even, corner_across[k, c], corner_mate[k, c])
        corner = unpack_columns(*corner)
        return own, vert, horiz, corner

    wave = []
    for s in range(2):
        ry, rx = shifts[s]
        wave.append([pltpu.roll(pltpu.roll(probe[c], rx, 1), ry, 0) for c in range(2)])

    for k in range(slices):
        parts = [candidates(k, c) for c in range(2)]
        exit_wave = []
        for s in range(2):
            o = []
            for c in range(2):
                own, vert, horiz, corner = parts[c]
                picked = jnp.where(
                    row_own[s],
                    jnp.where(col_own[s], own, horiz),
                    jnp.where(col_own[s], vert, corner),
                )
                patches[k, s, c] = picked
                waves[k, s, c] = wave[s][c]
                o.append(picked)
            wr, wi = wave[s]
            exit_wave.append((wr * o[0] - wi * o[1], wr * o[1] + wi * o[0]))
        if k + 1 < slices:
            wave = two_sided(exit_wave, step, step_t)
        else:
            far = two_sided(exit_wave, dft, dft_t)

    grad = []
    for s in range(2):
        fr, fi = far[s]
        live = jnp.where(s < count[0, 0], 2.0, 0.0)
        scale = live * (1.0 - measured[s] * lax.rsqrt(fr * fr + fi * fi + 1.0))
        grad.append((scale * fr, scale * fi))
    for k in reversed(range(slices)):
        if k + 1 < slices:
            grad = two_sided(grad, step_t, step)
        else:
            grad = two_sided(grad, dft_t, dft)
        onto_object = [[], []]
        onto_wave = []
        for s in range(2):
            gr, gi = grad[s]
            wr, wi = waves[k, s, 0], waves[k, s, 1]
            pr, pi = patches[k, s, 0], patches[k, s, 1]
            onto_object[0].append(wr * gr + wi * gi)
            onto_object[1].append(wr * gi - wi * gr)
            onto_wave.append((pr * gr + pi * gi, pr * gi - pi * gr))
        grad = onto_wave
        for c in range(2):
            zero = jnp.zeros((N, N), jnp.float32)
            own, vert, horiz, corner = zero, zero, zero, zero
            for s in range(2):
                g = onto_object[c][s]
                inside = jnp.where(row_own[s], g, 0.0)
                outside = jnp.where(row_own[s], 0.0, g)
                own += jnp.where(col_own[s], inside, 0.0)
                horiz += jnp.where(col_own[s], 0.0, inside)
                vert += jnp.where(col_own[s], outside, 0.0)
                corner += jnp.where(col_own[s], 0.0, outside)
            own_out[k, c] = own
            vert_out[k, c] = vert
            horiz_out[k, c] = horiz
            corner_out[k, c] = corner

    for c in range(2):
        total = jnp.zeros((N, N), jnp.float32)
        for s in range(2):
            ry, rx = shifts[s]
            back_y = jnp.bitwise_and(N - ry, N - 1)
            back_x = jnp.bitwise_and(N - rx, N - 1)
            total += pltpu.roll(pltpu.roll(grad[s][c], back_x, 1), back_y, 0)
        probe_out[c] = total


def sides_kernel(horiz_in, corner_in, col_across, col_mate):
    low = lane_mask()
    col_even = jnp.concatenate([even("c")] * 2, axis=0)
    for k in range(horiz_in.shape[0]):
        for c in range(2):
            horiz, corner = turned_rows(horiz_in[k, c]), corner_in[k, c]
            to_left = jnp.where(low, horiz, pltpu.roll(corner, H, 1))
            to_right = jnp.where(low, pltpu.roll(horiz, H, 1), corner)
            col_across[k, c], col_mate[k, c] = sort(col_even, to_left, to_right)


def vertical_kernel(vert, col_across, col_mate, row_across, row_mate):
    low = lane_mask()
    row_even = even("x")
    col_even = jnp.concatenate([even("c")] * 2, axis=0)
    for k in range(vert.shape[0]):
        for c in range(2):
            from_left, from_right = sort(col_even, col_across[k, c], col_mate[k, c])
            add = jnp.where(low, pltpu.roll(from_left, H, 1), from_right)
            v = pltpu.roll(vert[k, c], H, 1) + add
            row_across[k, c], row_mate[k, c] = sort(row_even, v[:H], v[H:])


def final_kernel(own, col_across, col_mate, row_across, row_mate, out):
    low = lane_mask()
    row_even = even("x")
    col_even = jnp.concatenate([even("c")] * 2, axis=0)
    for k in range(own.shape[0]):
        for c in range(2):
            from_left, from_right = sort(col_even, col_across[k, c], col_mate[k, c])
            add = jnp.where(low, from_left, pltpu.roll(from_right, H, 1))
            v = jnp.concatenate(sort(row_even, row_across[k, c], row_mate[k, c]), axis=0)
            out[k, c] = turned_rows(pltpu.roll(own[k, c], H, 1)) + add + v


def call(kernel, outs, args, name, scalars=0, scratch=(), vmem=4, flops=0):
    spec = pl.BlockSpec(memory_space=pltpu.VMEM)
    smem = pl.BlockSpec(memory_space=pltpu.SMEM)
    return pl.pallas_call(
        kernel,
        out_shape=[jax.ShapeDtypeStruct(s, jnp.float32) for s in outs],
        in_specs=[smem] * scalars + [spec] * (len(args) - scalars),
        out_specs=[spec] * len(outs),
        scratch_shapes=list(scratch),
        compiler_params=pltpu.CompilerParams(vmem_limit_bytes=vmem * 1024 * 1024),
        cost_estimate=pl.CostEstimate(
            flops=flops,
            bytes_accessed=sum(4 * int(np.prod(s)) for s in outs) + sum(x.nbytes for x in args),
            transcendentals=0,
        ),
        name=name,
    )(*args)


def swap(across, mate, axis):
    size = lax.axis_size(axis)
    over = [(i, i + 1 if i % 2 else i - 1) for i in range(1, size - 1)]
    return lax.ppermute(across, axis, over), lax.ppermute(mate, axis, [(i, i ^ 1) for i in range(size)])


def exchange(x, axis):
    return lax.all_to_all(x, axis, 0, 0, tiled=True)


def gathered_sum(x, axis):
    n = lax.axis_size(axis)
    rows = x.shape[0]
    parts = exchange(jnp.broadcast_to(x, (n, *x.shape)).reshape(n * rows, N), axis)
    return parts.reshape(n, rows, N).sum(axis=0)


def per_device(object_field, probe_wave, positions, counts, measured):
    slices = object_field.shape[0]
    full = (slices, 2, N, N)
    half = (slices, 2, H, N)
    consts = jnp.asarray(constant_operands())
    with jax.named_scope("object_halo"):
        edges = call(edges_kernel, [half] * 4, (object_field,), "pack_edges")
        rows = swap(*edges[:2], ROW)
        cols = swap(*edges[2:], COL)
        corners = swap(*call(corners_kernel, [half] * 2, rows, "pack_corners"), COL)
    own, vert, horiz, corner, probe_sum = call(
        grad_kernel,
        [full, full, full, full, (2, N, N)],
        (
            positions, counts, object_field, *rows, *cols, *corners,
            probe_wave, measured[0, 0], consts,
        ),
        "slot_gradients",
        scalars=2,
        vmem=16,
        flops=16 * 6 * (2 * N) ** 3,
        scratch=[pltpu.VMEM((slices, 2, 2, N, N), jnp.float32) for _ in range(2)],
    )
    with jax.named_scope("gradient_halo"):
        cols = swap(*call(sides_kernel, [full] * 2, (horiz, corner), "pack_sides"), COL)
        rows = swap(*call(vertical_kernel, [half] * 2, (vert, *cols), "add_vertical"), ROW)
        (result,) = call(final_kernel, [full], (own, *cols, *rows), "add_own")
    with jax.named_scope("probe_sum"):
        near = ("x", "c")
        groups = lax.axis_size(near)
        part = exchange(probe_sum.reshape(2 * N, N), near)
        part = part.reshape(groups, 2 * N // groups, N).sum(axis=0)
        part = gathered_sum(part, "y")
        part = gathered_sum(part, "z")
        spread = jnp.broadcast_to(part, (groups, *part.shape)).reshape(2 * N, N)
        probe_grad = exchange(spread, near).reshape(2, N, N)
    return (result, probe_grad)


def solution(mesh):
    rows, cols = mesh.devices.shape
    devices = mesh.devices.reshape(rows // CHIPS_X, CHIPS_X, cols // CORES, CORES)
    fine = Mesh(devices, ("z", "x", "y", "c"))
    in_specs = (
        P(None, None, ROW, COL),
        P(),
        P(ROW, COL, None, None),
        P(ROW, COL),
        P(ROW, COL, None, None, None),
    )
    out_specs = (P(None, None, ROW, COL), P())
    return jax.shard_map(
        per_device, mesh=fine, in_specs=in_specs, out_specs=out_specs, check_vma=False
    )
```

```python
import jax
import jax.numpy as jnp
import ml_dtypes
import numpy as np
from jax import lax
from jax.experimental import pallas as pl
from jax.experimental.pallas import tpu as pltpu
from jax.sharding import Mesh, PartitionSpec as P

FRESNEL = 0.01
N = 128
H = N // 2
CHIPS_X = 4
CORES = 2
ROW = ("z", "x")
COL = ("y", "c")


def constant_operands():
    k = np.arange(N)
    dft = np.exp(-2j * np.pi / N * (np.outer(k, k) % N)) / np.sqrt(N)
    u = np.where(k < H, k, k - N).astype(np.float64)
    p = np.exp(-1j * FRESNEL * u * u)
    step = dft.conj() @ (p[:, None] * dft)
    out = []
    for m in (step.real, step.imag, dft.real, dft.imag):
        high = m.astype(ml_dtypes.bfloat16)
        out += [high, (m - high.astype(np.float64)).astype(ml_dtypes.bfloat16)]
    return np.stack(out)


def split(x):
    high = x.astype(jnp.bfloat16)
    return high, (x - high.astype(jnp.float32)).astype(jnp.bfloat16)


def dot(a, b):
    return jnp.dot(a, b, preferred_element_type=jnp.float32)


def two_sided(wave, right, left):
    x = jnp.concatenate([jnp.concatenate(w, axis=1) for w in wave], axis=0)
    xh, xl = split(x)
    rh, rl = right
    z = dot(jnp.concatenate([xh, xl, xh], axis=1), jnp.concatenate([rh, rh, rl], axis=0))
    z = jnp.concatenate(
        [
            jnp.concatenate([z[:N, :N], z[N:, :N]], axis=1),
            jnp.concatenate([z[:N, N:], z[N:, N:]], axis=1),
        ],
        axis=0,
    )
    zh, zl = split(z)
    lh, ll = left
    y = dot(jnp.concatenate([lh, ll, lh], axis=1), jnp.concatenate([zh, zh, zl], axis=0))
    return [(y[:N, :N], y[N:, :N]), (y[:N, N:], y[N:, N:])]


def lane_mask():
    return lax.broadcasted_iota(jnp.int32, (N, N), 1) < H


def pack_columns(x):
    low = lax.broadcasted_iota(jnp.int32, (H, N), 1) < H
    upper, lower = x[:H], x[H:]
    to_right = jnp.where(low, pltpu.roll(upper, H, 1), lower)
    return jnp.where(low, upper, pltpu.roll(lower, H, 1)), to_right


def unpack_columns(from_left, from_right):
    low = lax.broadcasted_iota(jnp.int32, (H, N), 1) < H
    upper = jnp.where(low, from_left, pltpu.roll(from_right, H, 1))
    lower = jnp.where(low, pltpu.roll(from_left, H, 1), from_right)
    return jnp.concatenate([upper, lower], axis=0)


def even(axis):
    return jnp.full((H, N), jnp.bitwise_and(lax.axis_index(axis), 1), jnp.int32) == 0


def sort(is_even, before, after):
    return jnp.where(is_even, before, after), jnp.where(is_even, after, before)


def edges_kernel(tile, row_across, row_mate, col_across, col_mate):
    row_even, col_even = even("x"), even("c")
    for k in range(tile.shape[0]):
        for c in range(2):
            t = tile[k, c]
            row_across[k, c], row_mate[k, c] = sort(row_even, t[:H], t[H:])
            col_across[k, c], col_mate[k, c] = sort(col_even, *pack_columns(t))


def corners_kernel(row_across, row_mate, col_across, col_mate):
    row_even, col_even = even("x"), even("c")
    for k in range(row_across.shape[0]):
        for c in range(2):
            v = jnp.concatenate(sort(row_even, row_across[k, c], row_mate[k, c]), axis=0)
            col_across[k, c], col_mate[k, c] = sort(col_even, *pack_columns(v))


def turned_rows(x):
    return jnp.concatenate([x[H:], x[:H]], axis=0)


def grad_kernel(
    pos, count, tile, row_across, row_mate, col_across, col_mate, corner_across, corner_mate,
    probe, measured, consts,
    own_out, vert_out, horiz_out, corner_out, probe_out, patches, waves,
):
    slices = tile.shape[0]
    row_even, col_even = even("x"), even("c")
    rows = lax.broadcasted_iota(jnp.int32, (N, N), 0)
    cols = lax.broadcasted_iota(jnp.int32, (N, N), 1)
    def operator(i):
        right, left = [], []
        for term in range(2):
            real, imag = consts[4 * i + term], consts[4 * i + 2 + term]
            row = jnp.concatenate([real, imag], axis=1)
            col = jnp.concatenate([real, -imag], axis=1)
            right.append(jnp.concatenate([row, jnp.concatenate([-imag, real], axis=1)], axis=0))
            left.append(jnp.concatenate([col, jnp.concatenate([imag, real], axis=1)], axis=0))
        return right, left

    (step, step_t), (dft, dft_t) = operator(0), operator(1)

    shifts, row_own, col_own = [], [], []
    for s in range(2):
        ry = jnp.bitwise_and(pos[0, 0, s, 0], N - 1)
        rx = jnp.bitwise_and(pos[0, 0, s, 1], N - 1)
        shifts.append((ry, rx))
        row_own.append((rows < H) == (rows < ry))
        col_own.append((cols < H) == (cols < rx))

    def candidates(k, c):
        own = pltpu.roll(turned_rows(tile[k, c]), H, 1)
        vert = sort(row_even, row_across[k, c], row_mate[k, c])
        vert = pltpu.roll(jnp.concatenate(vert, axis=0), H, 1)
        horiz = sort(col_even, col_across[k, c], col_mate[k, c])
        horiz = turned_rows(unpack_columns(*horiz))
        corner = sort(col_even, corner_across[k, c], corner_mate[k, c])
        corner = unpack_columns(*corner)
        return own, vert, horiz, corner

    wave = []
    for s in range(2):
        ry, rx = shifts[s]
        wave.append([pltpu.roll(pltpu.roll(probe[c], rx, 1), ry, 0) for c in range(2)])

    for k in range(slices):
        parts = [candidates(k, c) for c in range(2)]
        exit_wave = []
        for s in range(2):
            o = []
            for c in range(2):
                own, vert, horiz, corner = parts[c]
                picked = jnp.where(
                    row_own[s],
                    jnp.where(col_own[s], own, horiz),
                    jnp.where(col_own[s], vert, corner),
                )
                patches[k, s, c] = picked
                waves[k, s, c] = wave[s][c]
                o.append(picked)
            wr, wi = wave[s]
            exit_wave.append((wr * o[0] - wi * o[1], wr * o[1] + wi * o[0]))
        if k + 1 < slices:
            wave = two_sided(exit_wave, step, step_t)
        else:
            far = two_sided(exit_wave, dft, dft_t)

    grad = []
    for s in range(2):
        fr, fi = far[s]
        live = jnp.where(s < count[0, 0], 2.0, 0.0)
        scale = live * (1.0 - measured[s] * lax.rsqrt(fr * fr + fi * fi + 1.0))
        grad.append((scale * fr, scale * fi))
    for k in reversed(range(slices)):
        if k + 1 < slices:
            grad = two_sided(grad, step_t, step)
        else:
            grad = two_sided(grad, dft_t, dft)
        onto_object = [[], []]
        onto_wave = []
        for s in range(2):
            gr, gi = grad[s]
            wr, wi = waves[k, s, 0], waves[k, s, 1]
            pr, pi = patches[k, s, 0], patches[k, s, 1]
            onto_object[0].append(wr * gr + wi * gi)
            onto_object[1].append(wr * gi - wi * gr)
            onto_wave.append((pr * gr + pi * gi, pr * gi - pi * gr))
        grad = onto_wave
        for c in range(2):
            zero = jnp.zeros((N, N), jnp.float32)
            own, vert, horiz, corner = zero, zero, zero, zero
            for s in range(2):
                g = onto_object[c][s]
                inside = jnp.where(row_own[s], g, 0.0)
                outside = jnp.where(row_own[s], 0.0, g)
                own += jnp.where(col_own[s], inside, 0.0)
                horiz += jnp.where(col_own[s], 0.0, inside)
                vert += jnp.where(col_own[s], outside, 0.0)
                corner += jnp.where(col_own[s], 0.0, outside)
            own_out[k, c] = own
            vert_out[k, c] = vert
            horiz_out[k, c] = horiz
            corner_out[k, c] = corner

    for c in range(2):
        total = jnp.zeros((N, N), jnp.float32)
        for s in range(2):
            ry, rx = shifts[s]
            back_y = jnp.bitwise_and(N - ry, N - 1)
            back_x = jnp.bitwise_and(N - rx, N - 1)
            total += pltpu.roll(pltpu.roll(grad[s][c], back_x, 1), back_y, 0)
        probe_out[c] = total


def sides_kernel(horiz_in, corner_in, col_across, col_mate):
    low = lane_mask()
    col_even = jnp.concatenate([even("c")] * 2, axis=0)
    for k in range(horiz_in.shape[0]):
        for c in range(2):
            horiz, corner = turned_rows(horiz_in[k, c]), corner_in[k, c]
            to_left = jnp.where(low, horiz, pltpu.roll(corner, H, 1))
            to_right = jnp.where(low, pltpu.roll(horiz, H, 1), corner)
            col_across[k, c], col_mate[k, c] = sort(col_even, to_left, to_right)


def vertical_kernel(vert, col_across, col_mate, row_across, row_mate):
    low = lane_mask()
    row_even = even("x")
    col_even = jnp.concatenate([even("c")] * 2, axis=0)
    for k in range(vert.shape[0]):
        for c in range(2):
            from_left, from_right = sort(col_even, col_across[k, c], col_mate[k, c])
            add = jnp.where(low, pltpu.roll(from_left, H, 1), from_right)
            v = pltpu.roll(vert[k, c], H, 1) + add
            row_across[k, c], row_mate[k, c] = sort(row_even, v[:H], v[H:])


def final_kernel(own, col_across, col_mate, row_across, row_mate, out):
    low = lane_mask()
    row_even = even("x")
    col_even = jnp.concatenate([even("c")] * 2, axis=0)
    for k in range(own.shape[0]):
        for c in range(2):
            from_left, from_right = sort(col_even, col_across[k, c], col_mate[k, c])
            add = jnp.where(low, from_left, pltpu.roll(from_right, H, 1))
            v = jnp.concatenate(sort(row_even, row_across[k, c], row_mate[k, c]), axis=0)
            out[k, c] = turned_rows(pltpu.roll(own[k, c], H, 1)) + add + v


def call(kernel, outs, args, name, scalars=0, scratch=(), vmem=4, flops=0):
    spec = pl.BlockSpec(memory_space=pltpu.VMEM)
    smem = pl.BlockSpec(memory_space=pltpu.SMEM)
    return pl.pallas_call(
        kernel,
        out_shape=[jax.ShapeDtypeStruct(s, jnp.float32) for s in outs],
        in_specs=[smem] * scalars + [spec] * (len(args) - scalars),
        out_specs=[spec] * len(outs),
        scratch_shapes=list(scratch),
        compiler_params=pltpu.CompilerParams(vmem_limit_bytes=vmem * 1024 * 1024),
        cost_estimate=pl.CostEstimate(
            flops=flops,
            bytes_accessed=sum(4 * int(np.prod(s)) for s in outs) + sum(x.nbytes for x in args),
            transcendentals=0,
        ),
        name=name,
    )(*args)


def swap(across, mate, axis):
    size = lax.axis_size(axis)
    over = [(i, i + 1 if i % 2 else i - 1) for i in range(1, size - 1)]
    return lax.ppermute(across, axis, over), lax.ppermute(mate, axis, [(i, i ^ 1) for i in range(size)])


def exchange(x, axis):
    return lax.all_to_all(x, axis, 0, 0, tiled=True)


def sum_kernel(parts, out):
    total = parts[0]
    for i in range(1, parts.shape[0]):
        total += parts[i]
    for i in range(out.shape[0]):
        out[i] = total


def summed(parts, groups, copies):
    rows = parts.shape[0] // groups
    args = (parts.reshape(groups, rows, N),)
    (out,) = call(sum_kernel, [(copies, rows, N)], args, "sum_parts", flops=20 * 10**9)
    return out.reshape(copies * rows, N)


def per_device(object_field, probe_wave, positions, counts, measured):
    slices = object_field.shape[0]
    full = (slices, 2, N, N)
    half = (slices, 2, H, N)
    consts = jnp.asarray(constant_operands())
    with jax.named_scope("object_halo"):
        edges = call(edges_kernel, [half] * 4, (object_field,), "pack_edges")
        rows = swap(*edges[:2], ROW)
        cols = swap(*edges[2:], COL)
        corners = swap(*call(corners_kernel, [half] * 2, rows, "pack_corners"), COL)
    own, vert, horiz, corner, probe_sum = call(
        grad_kernel,
        [full, full, full, full, (2, N, N)],
        (
            positions, counts, object_field, *rows, *cols, *corners,
            probe_wave, measured[0, 0], consts,
        ),
        "slot_gradients",
        scalars=2,
        vmem=16,
        flops=16 * 6 * (2 * N) ** 3,
        scratch=[pltpu.VMEM((slices, 2, 2, N, N), jnp.float32) for _ in range(2)],
    )
    plane, across_planes = ("x", "y"), ("z", "c")
    groups, copies = lax.axis_size(plane), lax.axis_size(across_planes)
    with jax.named_scope("probe_sum_plane"):
        parts = exchange(probe_sum.reshape(2 * N, N), plane)
    with jax.named_scope("gradient_columns"):
        cols = swap(*call(sides_kernel, [full] * 2, (horiz, corner), "pack_sides"), COL)
    with jax.named_scope("probe_sum_z"):
        parts = exchange(summed(parts, groups, copies), across_planes)
    with jax.named_scope("gradient_rows"):
        rows = swap(*call(vertical_kernel, [half] * 2, (vert, *cols), "add_vertical"), ROW)
        (result,) = call(final_kernel, [full], (own, *cols, *rows), "add_own")
    with jax.named_scope("probe_sum_gather"):
        probe_grad = exchange(summed(parts, copies, groups), plane).reshape(2, N, N)
    return (result, probe_grad)


def solution(mesh):
    rows, cols = mesh.devices.shape
    devices = mesh.devices.reshape(rows // CHIPS_X, CHIPS_X, cols // CORES, CORES)
    fine = Mesh(devices, ("z", "x", "y", "c"))
    in_specs = (
        P(None, None, ROW, COL),
        P(),
        P(ROW, COL, None, None),
        P(ROW, COL),
        P(ROW, COL, None, None, None),
    )
    out_specs = (P(None, None, ROW, COL), P())
    return jax.shard_map(
        per_device, mesh=fine, in_specs=in_specs, out_specs=out_specs, check_vma=False
    )
```

```python
import jax
import jax.numpy as jnp
import ml_dtypes
import numpy as np
from jax import lax
from jax.experimental import pallas as pl
from jax.experimental.pallas import tpu as pltpu
from jax.sharding import Mesh, PartitionSpec as P

FRESNEL = 0.01
N = 128
H = N // 2
CHIPS_X = 4
CORES = 2
ROW = ("z", "x")
COL = ("y", "c")


def constant_operands():
    k = np.arange(N)
    dft = np.exp(-2j * np.pi / N * (np.outer(k, k) % N)) / np.sqrt(N)
    u = np.where(k < H, k, k - N).astype(np.float64)
    p = np.exp(-1j * FRESNEL * u * u)
    step = dft.conj() @ (p[:, None] * dft)
    out = []
    for m in (step.real, step.imag, dft.real, dft.imag):
        high = m.astype(ml_dtypes.bfloat16)
        out += [high, (m - high.astype(np.float64)).astype(ml_dtypes.bfloat16)]
    return np.stack(out)


def split(x):
    high = x.astype(jnp.bfloat16)
    return high, (x - high.astype(jnp.float32)).astype(jnp.bfloat16)


def dot(a, b):
    return jnp.dot(a, b, preferred_element_type=jnp.float32)


def two_sided(wave, right, left):
    x = jnp.concatenate([jnp.concatenate(w, axis=1) for w in wave], axis=0)
    xh, xl = split(x)
    rh, rl = right
    z = dot(jnp.concatenate([xh, xl, xh], axis=1), jnp.concatenate([rh, rh, rl], axis=0))
    z = jnp.concatenate(
        [
            jnp.concatenate([z[:N, :N], z[N:, :N]], axis=1),
            jnp.concatenate([z[:N, N:], z[N:, N:]], axis=1),
        ],
        axis=0,
    )
    zh, zl = split(z)
    lh, ll = left
    y = dot(jnp.concatenate([lh, ll, lh], axis=1), jnp.concatenate([zh, zh, zl], axis=0))
    return [(y[:N, :N], y[N:, :N]), (y[:N, N:], y[N:, N:])]


def lane_mask():
    return lax.broadcasted_iota(jnp.int32, (N, N), 1) < H


def pack_columns(x):
    low = lax.broadcasted_iota(jnp.int32, (H, N), 1) < H
    upper, lower = x[:H], x[H:]
    to_right = jnp.where(low, pltpu.roll(upper, H, 1), lower)
    return jnp.where(low, upper, pltpu.roll(lower, H, 1)), to_right


def unpack_columns(from_left, from_right):
    low = lax.broadcasted_iota(jnp.int32, (H, N), 1) < H
    upper = jnp.where(low, from_left, pltpu.roll(from_right, H, 1))
    lower = jnp.where(low, pltpu.roll(from_left, H, 1), from_right)
    return jnp.concatenate([upper, lower], axis=0)


def even(axis):
    return jnp.full((H, N), jnp.bitwise_and(lax.axis_index(axis), 1), jnp.int32) == 0


def sort(is_even, before, after):
    return jnp.where(is_even, before, after), jnp.where(is_even, after, before)


def rows_kernel(tile, row_across, row_mate, arrived):
    odd = jnp.bitwise_and(lax.axis_index("x"), 1)
    copies = []
    for i, (half, out) in enumerate(((odd, row_across), (1 - odd, row_mate))):
        rows = pl.ds(pl.multiple_of(half * H, H), H)
        copies.append(pltpu.make_async_copy(tile.at[:, :, rows, :], out, arrived.at[i]))
        copies[-1].start()
    for copy in copies:
        copy.wait()


def columns_kernel(tile, col_across, col_mate):
    col_even = even("c")
    for k in range(tile.shape[0]):
        for c in range(2):
            col_across[k, c], col_mate[k, c] = sort(col_even, *pack_columns(tile[k, c]))


def corners_kernel(row_across, row_mate, col_across, col_mate):
    row_even, col_even = even("x"), even("c")
    for k in range(row_across.shape[0]):
        for c in range(2):
            v = jnp.concatenate(sort(row_even, row_across[k, c], row_mate[k, c]), axis=0)
            col_across[k, c], col_mate[k, c] = sort(col_even, *pack_columns(v))


def turned_rows(x):
    return jnp.concatenate([x[H:], x[:H]], axis=0)


def grad_kernel(
    pos, count, tile, row_across, row_mate, col_across, col_mate, corner_across, corner_mate,
    probe, measured, consts,
    own_out, vert_out, horiz_out, corner_out, probe_out, patches, waves,
):
    slices = tile.shape[0]
    row_even, col_even = even("x"), even("c")
    rows = lax.broadcasted_iota(jnp.int32, (N, N), 0)
    cols = lax.broadcasted_iota(jnp.int32, (N, N), 1)
    def operator(i):
        right, left = [], []
        for term in range(2):
            real, imag = consts[4 * i + term], consts[4 * i + 2 + term]
            row = jnp.concatenate([real, imag], axis=1)
            col = jnp.concatenate([real, -imag], axis=1)
            right.append(jnp.concatenate([row, jnp.concatenate([-imag, real], axis=1)], axis=0))
            left.append(jnp.concatenate([col, jnp.concatenate([imag, real], axis=1)], axis=0))
        return right, left

    (step, step_t), (dft, dft_t) = operator(0), operator(1)

    shifts, row_own, col_own = [], [], []
    for s in range(2):
        ry = jnp.bitwise_and(pos[0, 0, s, 0], N - 1)
        rx = jnp.bitwise_and(pos[0, 0, s, 1], N - 1)
        shifts.append((ry, rx))
        row_own.append((rows < H) == (rows < ry))
        col_own.append((cols < H) == (cols < rx))

    def candidates(k, c):
        own = pltpu.roll(turned_rows(tile[k, c]), H, 1)
        vert = sort(row_even, row_across[k, c], row_mate[k, c])
        vert = pltpu.roll(jnp.concatenate(vert, axis=0), H, 1)
        horiz = sort(col_even, col_across[k, c], col_mate[k, c])
        horiz = turned_rows(unpack_columns(*horiz))
        corner = sort(col_even, corner_across[k, c], corner_mate[k, c])
        corner = unpack_columns(*corner)
        return own, vert, horiz, corner

    wave = []
    for s in range(2):
        ry, rx = shifts[s]
        wave.append([pltpu.roll(pltpu.roll(probe[c], rx, 1), ry, 0) for c in range(2)])

    for k in range(slices):
        parts = [candidates(k, c) for c in range(2)]
        exit_wave = []
        for s in range(2):
            o = []
            for c in range(2):
                own, vert, horiz, corner = parts[c]
                picked = jnp.where(
                    row_own[s],
                    jnp.where(col_own[s], own, horiz),
                    jnp.where(col_own[s], vert, corner),
                )
                patches[k, s, c] = picked
                waves[k, s, c] = wave[s][c]
                o.append(picked)
            wr, wi = wave[s]
            exit_wave.append((wr * o[0] - wi * o[1], wr * o[1] + wi * o[0]))
        if k + 1 < slices:
            wave = two_sided(exit_wave, step, step_t)
        else:
            far = two_sided(exit_wave, dft, dft_t)

    grad = []
    for s in range(2):
        fr, fi = far[s]
        live = jnp.where(s < count[0, 0], 2.0, 0.0)
        scale = live * (1.0 - measured[s] * lax.rsqrt(fr * fr + fi * fi + 1.0))
        grad.append((scale * fr, scale * fi))
    for k in reversed(range(slices)):
        if k + 1 < slices:
            grad = two_sided(grad, step_t, step)
        else:
            grad = two_sided(grad, dft_t, dft)
        onto_object = [[], []]
        onto_wave = []
        for s in range(2):
            gr, gi = grad[s]
            wr, wi = waves[k, s, 0], waves[k, s, 1]
            pr, pi = patches[k, s, 0], patches[k, s, 1]
            onto_object[0].append(wr * gr + wi * gi)
            onto_object[1].append(wr * gi - wi * gr)
            onto_wave.append((pr * gr + pi * gi, pr * gi - pi * gr))
        grad = onto_wave
        for c in range(2):
            zero = jnp.zeros((N, N), jnp.float32)
            own, vert, horiz, corner = zero, zero, zero, zero
            for s in range(2):
                g = onto_object[c][s]
                inside = jnp.where(row_own[s], g, 0.0)
                outside = jnp.where(row_own[s], 0.0, g)
                own += jnp.where(col_own[s], inside, 0.0)
                horiz += jnp.where(col_own[s], 0.0, inside)
                vert += jnp.where(col_own[s], outside, 0.0)
                corner += jnp.where(col_own[s], 0.0, outside)
            own_out[k, c] = own
            vert_out[k, c] = vert
            horiz_out[k, c] = horiz
            corner_out[k, c] = corner

    for c in range(2):
        total = jnp.zeros((N, N), jnp.float32)
        for s in range(2):
            ry, rx = shifts[s]
            back_y = jnp.bitwise_and(N - ry, N - 1)
            back_x = jnp.bitwise_and(N - rx, N - 1)
            total += pltpu.roll(pltpu.roll(grad[s][c], back_x, 1), back_y, 0)
        probe_out[c] = total


def sides_kernel(horiz_in, corner_in, col_across, col_mate):
    low = lane_mask()
    col_even = jnp.concatenate([even("c")] * 2, axis=0)
    for k in range(horiz_in.shape[0]):
        for c in range(2):
            horiz, corner = turned_rows(horiz_in[k, c]), corner_in[k, c]
            to_left = jnp.where(low, horiz, pltpu.roll(corner, H, 1))
            to_right = jnp.where(low, pltpu.roll(horiz, H, 1), corner)
            col_across[k, c], col_mate[k, c] = sort(col_even, to_left, to_right)


def vertical_kernel(vert, col_across, col_mate, row_across, row_mate):
    low = lane_mask()
    row_even = even("x")
    col_even = jnp.concatenate([even("c")] * 2, axis=0)
    for k in range(vert.shape[0]):
        for c in range(2):
            from_left, from_right = sort(col_even, col_across[k, c], col_mate[k, c])
            add = jnp.where(low, pltpu.roll(from_left, H, 1), from_right)
            v = pltpu.roll(vert[k, c], H, 1) + add
            row_across[k, c], row_mate[k, c] = sort(row_even, v[:H], v[H:])


def final_kernel(own, col_across, col_mate, row_across, row_mate, out):
    low = lane_mask()
    row_even = even("x")
    col_even = jnp.concatenate([even("c")] * 2, axis=0)
    for k in range(own.shape[0]):
        for c in range(2):
            from_left, from_right = sort(col_even, col_across[k, c], col_mate[k, c])
            add = jnp.where(low, from_left, pltpu.roll(from_right, H, 1))
            v = jnp.concatenate(sort(row_even, row_across[k, c], row_mate[k, c]), axis=0)
            out[k, c] = turned_rows(pltpu.roll(own[k, c], H, 1)) + add + v


def call(kernel, outs, args, name, scalars=0, where=None, scratch=(), vmem=4, flops=0):
    spec = pl.BlockSpec(memory_space=pltpu.VMEM)
    smem = pl.BlockSpec(memory_space=pltpu.SMEM)
    return pl.pallas_call(
        kernel,
        out_shape=[jax.ShapeDtypeStruct(s, jnp.float32) for s in outs],
        in_specs=[smem] * scalars + [where or spec] * (len(args) - scalars),
        out_specs=[spec] * len(outs),
        scratch_shapes=list(scratch),
        compiler_params=pltpu.CompilerParams(vmem_limit_bytes=vmem * 1024 * 1024),
        cost_estimate=pl.CostEstimate(
            flops=flops,
            bytes_accessed=sum(4 * int(np.prod(s)) for s in outs) + sum(x.nbytes for x in args),
            transcendentals=0,
        ),
        name=name,
    )(*args)


def swap(across, mate, axis):
    size = lax.axis_size(axis)
    over = [(i, i + 1 if i % 2 else i - 1) for i in range(1, size - 1)]
    return lax.ppermute(across, axis, over), lax.ppermute(mate, axis, [(i, i ^ 1) for i in range(size)])


def exchange(x, axis):
    return lax.all_to_all(x, axis, 0, 0, tiled=True)


def sum_kernel(parts, out):
    total = parts[0]
    for i in range(1, parts.shape[0]):
        total += parts[i]
    for i in range(out.shape[0]):
        out[i] = total


def summed(parts, groups, copies):
    rows = parts.shape[0] // groups
    args = (parts.reshape(groups, rows, N),)
    (out,) = call(sum_kernel, [(copies, rows, N)], args, "sum_parts", flops=20 * 10**9)
    return out.reshape(copies * rows, N)


def per_device(object_field, probe_wave, positions, counts, measured):
    slices = object_field.shape[0]
    full = (slices, 2, N, N)
    half = (slices, 2, H, N)
    consts = jnp.asarray(constant_operands())
    with jax.named_scope("object_halo"):
        rows = call(
            rows_kernel, [half] * 2, (pltpu.with_memory_space_constraint(object_field, pltpu.HBM),), "pick_rows",
            where=pl.BlockSpec(memory_space=pltpu.HBM), scratch=[pltpu.SemaphoreType.DMA((2,))],
        )
        rows = swap(*rows, ROW)
        cols = swap(*call(columns_kernel, [half] * 2, (object_field,), "pack_columns"), COL)
        corners = swap(*call(corners_kernel, [half] * 2, rows, "pack_corners"), COL)
    own, vert, horiz, corner, probe_sum = call(
        grad_kernel,
        [full, full, full, full, (2, N, N)],
        (
            positions, counts, object_field, *rows, *cols, *corners,
            probe_wave, measured[0, 0], consts,
        ),
        "slot_gradients",
        scalars=2,
        vmem=16,
        flops=16 * 6 * (2 * N) ** 3,
        scratch=[pltpu.VMEM((slices, 2, 2, N, N), jnp.float32) for _ in range(2)],
    )
    plane, across_planes = ("x", "y"), ("z", "c")
    groups, copies = lax.axis_size(plane), lax.axis_size(across_planes)
    with jax.named_scope("probe_sum_plane"):
        parts = exchange(probe_sum.reshape(2 * N, N), plane)
    with jax.named_scope("gradient_columns"):
        cols = swap(*call(sides_kernel, [full] * 2, (horiz, corner), "pack_sides"), COL)
    with jax.named_scope("probe_sum_z"):
        parts = exchange(summed(parts, groups, copies), across_planes)
    with jax.named_scope("gradient_rows"):
        rows = swap(*call(vertical_kernel, [half] * 2, (vert, *cols), "add_vertical"), ROW)
        (result,) = call(final_kernel, [full], (own, *cols, *rows), "add_own")
    with jax.named_scope("probe_sum_gather"):
        probe_grad = exchange(summed(parts, copies, groups), plane).reshape(2, N, N)
    return (result, probe_grad)


def solution(mesh):
    rows, cols = mesh.devices.shape
    devices = mesh.devices.reshape(rows // CHIPS_X, CHIPS_X, cols // CORES, CORES)
    fine = Mesh(devices, ("z", "x", "y", "c"))
    in_specs = (
        P(None, None, ROW, COL),
        P(),
        P(ROW, COL, None, None),
        P(ROW, COL),
        P(ROW, COL, None, None, None),
    )
    out_specs = (P(None, None, ROW, COL), P())
    return jax.shard_map(
        per_device, mesh=fine, in_specs=in_specs, out_specs=out_specs, check_vma=False
    )
```
